256 devices in a mesh: lon: 8 (over y, core), lat: 16 (over z_hi, x), lev: 2 (over z_lo).
Axes of the slice: x: 4, y: 4, z: 8 (z_hi: 4, z_lo: 2; z = z_hi * 2 + z_lo), core: 2. Of those that a mesh axis runs over, the one named last changes fastest.
Arguments:
- fields_grid: float32 [6, 2, 1024, 8192], P(None, 'lev', 'lat', 'lon'), may hold values from -6 to 6
- hermite_proj: float32 [1024, 1024], P('lat'), may hold values from -0.1875 to 0.1875
Outputs:
- spectrum: float32 [1024, 6, 2, 4096], P('lat', None, 'lev', 'lon')
The draws below stay inside these ranges and needn't reach their ends.
All inputs are finite; a program needn't handle non-finite values.
Results may differ from the reference program's by a relative error of at most 0.00007.
Values sent between devices are 32-bit elements; how exact they have to be, the bound alone decides.
A program may use at most 128 MiB of HBM per device.

```python
import math
import jax
import jax.numpy as jnp
from jax import lax

FIELDS = 6
NLON = 8192
NLAT = 1024
MODES = 1024
KZ = 2048
LEV = 2


def block_scale(key, extent, cuts, low, top_value):
    def one(position, shards_of):
        heights = jax.random.uniform(jax.random.fold_in(jax.random.fold_in(key, 6), position), (shards_of,), jnp.float32, low / len(cuts), top_value / len(cuts))
        return jnp.repeat(jnp.exp(heights), extent[position] // shards_of).reshape((-1,) + (1,) * (len(extent) - position - 1))

    loudness = one(*cuts[0])
    for cut in cuts[1:]:
        loudness = loudness * one(*cut)
    return loudness


def scatter_about(rng, shape, scale, most, split=(), held_as=jnp.bfloat16):
    array = jax.random.normal(rng, shape, jnp.float32) * scale
    if len(split) > 0:
        array = block_scale(rng, shape, split, -0.22, 0.18) * array
    return jnp.clip(array, min=-most, max=most).astype(held_as)


def setup_inputs(seed: int = 0) -> dict:
    splits = jax.random.split(jax.random.key(seed), 3)
    fields_grid = scatter_about(splits[0], (FIELDS, LEV, NLAT, NLON), 1.0, 6.0, ((1, 2), (2, 16), (3, 8)), jnp.float32)
    hermite_proj = scatter_about(splits[1], (NLAT, MODES), NLAT ** -0.5, 0.1875, ((0, 16),), jnp.float32)
    return {"fields_grid": fields_grid, "hermite_proj": hermite_proj}


def pad_levels(field):
    return jnp.pad(field, ((1, 1), (0, 0), (0, 0)))

def slope_levels(field):
    padded = pad_levels(field)
    return 0.5 * (padded[2:] - padded[:-2])

def bend_levels(field):
    padded = pad_levels(field)
    return padded[2:] - 2.0 * field + padded[:-2]

def zonal_one(product):
    coeffs = jnp.fft.rfft(product, axis=-1)[..., :KZ]
    scale_factor = 1.0 / math.sqrt(NLON)
    joined = jnp.concatenate([jnp.real(coeffs), jnp.imag(coeffs)], axis=-1) * scale_factor
    return joined.astype(jnp.float32)

def reference(fields_grid, hermite_proj):
    zonal_wind = fields_grid[0]
    merid_wind = fields_grid[1]
    vert_wind = fields_grid[2]
    theta_field = fields_grid[3]
    humidity = fields_grid[4]
    geopotential = fields_grid[5]
    products = jnp.stack([zonal_wind * geopotential, zonal_wind * merid_wind, zonal_wind * humidity, merid_wind * theta_field, vert_wind * slope_levels(zonal_wind), vert_wind * slope_levels(theta_field) - 0.25 * bend_levels(humidity)])
    zonal = lax.map(zonal_one, products)
    return jnp.einsum('fkys,yn->nfks', zonal, hermite_proj, precision=lax.Precision.HIGHEST)
```

```python
import functools
import math

import jax
import jax.numpy as jnp
import ml_dtypes
import numpy as np
from jax import lax
from jax.experimental import pallas as pl
from jax.experimental.pallas import tpu as pltpu
from jax.sharding import PartitionSpec as P

MESH = pl.DeviceIdType.MESH
F32 = jnp.float32
BF16 = jnp.bfloat16
NLON = 8192
STEPS = 3


def split_np(table):
    high = table.astype(np.float32).astype(ml_dtypes.bfloat16)
    low = (table - high.astype(np.float64)).astype(np.float32).astype(ml_dtypes.bfloat16)
    return high, low


def tables():
    q = np.arange(64)
    p = np.arange(128)
    high_m = np.arange(32)
    first = 2.0 * np.pi * (np.outer(q, q) % 64) / 64
    first = np.concatenate([np.cos(first), -np.sin(first)], axis=0)
    f_high, f_low = split_np(first)
    first_cat = np.concatenate([f_high, f_low, f_high], axis=1)
    angle = 2.0 * np.pi * np.outer(q, p) / NLON
    twiddle = np.concatenate([np.cos(angle), np.sin(angle)], axis=0).astype(np.float32)
    second = 2.0 * np.pi * (np.outer(high_m, p) % 128) / 128
    cos_b, sin_b = np.cos(second), np.sin(second)
    second = np.concatenate(
        [np.concatenate([cos_b, sin_b], axis=1), np.concatenate([-sin_b, cos_b], axis=1)], axis=0
    ) / math.sqrt(NLON)
    s_high, s_low = split_np(second)
    second_cat = np.concatenate([s_high, s_low], axis=0)
    return first_cat, twiddle, second_cat


def split(value):
    high = value.astype(BF16)
    low = (value - high.astype(F32)).astype(BF16)
    return high, low


def wait_bytes(ref, sem):
    pltpu.make_async_copy(ref, ref, sem).wait()


def kernel(
    fields, herm, first_ref, twiddle_ref, second_ref, out_ref,
    halo, xs, xr, b_hi, b_lo, zs, zr, zct, pbuf, p_hi, p_lo, outs, gath,
    halo_send, halo_recv, lon_send, lon_recv, in_send, in_recv, out_send, out_recv,
    p_send, pz_recv, px_recv, pc_recv, round_two,
):
    lon = lax.axis_index("lon")
    lat = lax.axis_index("lat")
    lev = lax.axis_index("lev")
    yy, core = lon // 2, lax.rem(lon, 2)
    zz, xx = lat // 4, lax.rem(lat, 4)
    half, l8 = lax.rem(lat, 2), lat // 2
    other = 1 - lev

    own_rows = pl.ds(pl.multiple_of(lat * 64, 64), 64)
    for col in range(4):
        lanes = pl.ds(pl.multiple_of(core * 512 + col * 128, 128), 128)
        pltpu.make_async_copy(herm.at[:, lanes], pbuf.at[core, col, own_rows], pc_recv.at[1]).start()

    barrier = pltpu.get_barrier_semaphore()
    pl.semaphore_signal(barrier, inc=1, device_id=(lon, lat, other), device_id_type=MESH)
    for off in range(1, 8):
        pl.semaphore_signal(
            barrier, inc=1, device_id=(lax.rem(lon + off, 8), lat, lev), device_id_type=MESH
        )
    for off in range(1, 16):
        pl.semaphore_signal(
            barrier, inc=1, device_id=(lon, lax.rem(lat + off, 16), lev), device_id_type=MESH
        )
    pl.semaphore_wait(barrier, 23)

    halo_copies = []
    for slot, field in enumerate((2, 4)):
        copy = pltpu.make_async_remote_copy(
            src_ref=fields.at[field, 0], dst_ref=halo.at[slot],
            send_sem=halo_send.at[slot], recv_sem=halo_recv.at[slot],
            device_id=(lon, lat, other), device_id_type=MESH,
        )
        copy.start()
        halo_copies.append(copy)

    def make_products(dst_field, compute):
        @pl.loop(0, 8)
        def _(yb):
            rows = pl.ds(pl.multiple_of(yb * 8, 8), 8)
            value = compute(rows)
            for t in range(8):
                xs[pl.ds(dst_field * 512 + yb * 64 + t, 8, stride=8), :] = value[:, t * 128:(t + 1) * 128]

    def send_lon(step, to_core):
        field = 3 * to_core + step
        for dy in range(4):
            peer_y = lax.rem(yy + dy, 4)
            rows = pl.ds(pl.multiple_of(field * 512 + peer_y * 128, 128), 128)

            def remote():
                pltpu.make_async_remote_copy(
                    src_ref=xs.at[rows], dst_ref=xr.at[step, lon],
                    send_sem=lon_send.at[step], recv_sem=lon_recv.at[step],
                    device_id=(peer_y * 2 + to_core, lat, lev), device_id_type=MESH,
                ).start()

            if dy:
                remote()
            else:
                @pl.when(core != to_core)
                def _():
                    remote()

                @pl.when(core == to_core)
                def _():
                    pltpu.make_async_copy(xs.at[rows], xr.at[step, lon], lon_recv.at[step]).start()

    make_products(0, lambda r: fields[0, 0, r, :] * fields[5, 0, r, :])
    send_lon(0, 0)
    make_products(3, lambda r: fields[1, 0, r, :] * fields[3, 0, r, :])
    send_lon(0, 1)

    wait_bytes(herm.at[:, pl.ds(0, 512)], pc_recv.at[1])
    own = pbuf.at[core, :, own_rows]
    for dz in range(1, 4):
        pltpu.make_async_remote_copy(
            src_ref=own, dst_ref=own, send_sem=p_send.at[0], recv_sem=pz_recv.at[dz],
            device_id=(lon, lax.rem(zz + dz, 4) * 4 + xx, lev), device_id_type=MESH,
        ).start()
    for dx in range(1, 4):
        pltpu.make_async_remote_copy(
            src_ref=own, dst_ref=own, send_sem=p_send.at[1], recv_sem=px_recv.at[0, dx],
            device_id=(lon, zz * 4 + lax.rem(xx + dx, 4), lev), device_id_type=MESH,
        ).start()

    make_products(1, lambda r: fields[0, 0, r, :] * fields[1, 0, r, :])
    send_lon(1, 0)
    sign = jnp.where(lev == 0, F32(-0.5), F32(0.5))
    halo_copies[0].wait_recv()
    make_products(4, lambda r: halo[0, r, :] * (fields[0, 0, r, :] * sign))
    send_lon(1, 1)
    make_products(2, lambda r: fields[0, 0, r, :] * fields[4, 0, r, :])
    send_lon(2, 0)
    halo_copies[1].wait_recv()
    make_products(
        5,
        lambda r: halo[0, r, :] * (fields[3, 0, r, :] * sign)
        - 0.25 * (fields[4, 0, r, :] - 2.0 * halo[1, r, :]),
    )
    send_lon(2, 1)

    for dz in range(1, 4):
        wait_bytes(herm.at[:, pl.ds(0, 512)], pz_recv.at[dz])
        origin = lax.rem(zz + 4 - dz, 4) * 4 + xx
        rows = pl.ds(pl.multiple_of(origin * 64, 64), 64)
        for dx in range(1, 4):
            pltpu.make_async_remote_copy(
                src_ref=pbuf.at[core, :, rows], dst_ref=pbuf.at[core, :, rows],
                send_sem=p_send.at[1], recv_sem=px_recv.at[dz, dx],
                device_id=(lon, zz * 4 + lax.rem(xx + dx, 4), lev), device_id_type=MESH,
            ).start()

    def zonal(step):
        wait_bytes(xr.at[step], lon_recv.at[step])
        cos_t, sin_t = twiddle_ref[0:64, :], twiddle_ref[64:128, :]

        @pl.loop(0, 8)
        def _(u):
            cats = []
            for k in range(2):
                block = xr[step, :, pl.ds(pl.multiple_of(u * 16 + k * 8, 8), 8), :].reshape(64, 128)
                high, low = split(block)
                cats.append(jnp.concatenate([high, high, low], axis=0))
            cat = jnp.concatenate(cats, axis=1)
            first = jnp.dot(first_ref[...], cat, preferred_element_type=F32)
            res, ims = [], []
            for k in range(2):
                re = first[0:64, k * 128:(k + 1) * 128]
                im = first[64:128, k * 128:(k + 1) * 128]
                res.append((re * cos_t + im * sin_t).reshape(8, 8, 128))
                ims.append((im * cos_t - re * sin_t).reshape(8, 8, 128))
            rows = pl.ds(pl.multiple_of(u * 16, 16), 16)
            for part, pair in enumerate((res, ims)):
                high, low = split(jnp.concatenate(pair, axis=1))
                b_hi[:, rows, part * 128:(part + 1) * 128] = high
                b_lo[:, rows, part * 128:(part + 1) * 128] = low

        @pl.loop(0, 4)
        def _(u):
            pair = pl.ds(u * 2, 2)
            high = b_hi[pair].reshape(256, 256)
            low = b_lo[pair].reshape(256, 256)
            nt = (((1,), (1,)), ((), ()))
            one = lax.dot_general(second_ref[...], high, nt, preferred_element_type=F32)
            two = lax.dot_general(second_ref[0:64, :], low, nt, preferred_element_type=F32)
            both = one[0:64] + one[64:128] + two
            for k in range(2):
                zs[step, :, u * 2 + k] = both[:, k * 128:(k + 1) * 128].reshape(8, 8, 128)

    source = lat * 4 + yy
    my_g, my_s = source // 8, lax.rem(source, 8)

    def send_in(step):
        flip = jnp.logical_and(core == 1, step >= 1)
        to_lev = jnp.where(flip, other, lev)

        @pl.loop(0, 64)
        def _(j):
            dz, dx = j // 16, lax.rem(j // 8, 2)
            dy, dc = lax.rem(j // 2, 4), lax.rem(j, 2)
            to_x = lax.rem(xx + 2 * dx, 4) // 2 * 2 + core
            to_lat = lax.rem(zz + dz, 4) * 4 + to_x
            to_lon = lax.rem(yy + dy, 4) * 2 + lax.rem(core + dc, 2)
            mine = jnp.logical_and(jnp.logical_and(to_lat == lat, to_lon == lon), to_lev == lev)
            src = zs.at[step, to_lon, to_lat // 2]
            dst = zr.at[step, my_g, my_s]

            @pl.when(jnp.logical_not(mine))
            def _():
                pltpu.make_async_remote_copy(
                    src_ref=src, dst_ref=dst,
                    send_sem=in_send.at[step], recv_sem=in_recv.at[step],
                    device_id=(to_lon, to_lat, to_lev), device_id_type=MESH,
                ).start()

            @pl.when(mine)
            def _():
                pltpu.make_async_copy(src, dst, in_recv.at[step]).start()

    def wait_in_sends(step):
        flip = jnp.logical_and(core == 1, step >= 1)
        has_self = jnp.logical_and(half == core, jnp.logical_not(flip))

        @pl.when(has_self)
        def _():
            wait_bytes(zs.at[step, pl.ds(0, 7)], in_send.at[step])
            wait_bytes(zs.at[step, 0, pl.ds(0, 7)], in_send.at[step])

        @pl.when(jnp.logical_not(has_self))
        def _():
            wait_bytes(zs.at[step], in_send.at[step])

    zonal(0)
    for off in range(1, 16):
        pl.semaphore_signal(
            round_two, inc=1, device_id=(lon, lax.rem(lat + off, 16), lev), device_id_type=MESH
        )
    pl.semaphore_wait(round_two, 15)
    send_in(0)
    zonal(1)
    send_in(1)
    zonal(2)
    send_in(2)

    for dz in range(4):
        for dx in range(1, 4):
            wait_bytes(herm.at[:, pl.ds(0, 512)], px_recv.at[dz, dx])
    to_sibling = pltpu.make_async_remote_copy(
        src_ref=pbuf.at[core], dst_ref=pbuf.at[core],
        send_sem=p_send.at[2], recv_sem=pc_recv.at[0],
        device_id=(lon + 1 - 2 * core, lat, lev), device_id_type=MESH,
    )
    to_sibling.start()

    def prepare(which):
        @pl.loop(0, 64)
        def _(j):
            g, u = j // 8, lax.rem(j, 8)
            for col in range(4):
                pieces = [
                    pbuf[which, col, pl.ds(g * 128 + u * 2 + k, 8, stride=16), :]
                    for k in range(2)
                ]
                high, low = split(jnp.concatenate(pieces, axis=0))
                rows = pl.ds(pl.multiple_of(j * 16, 16), 16)
                p_hi[which, rows, col * 128:(col + 1) * 128] = high
                p_lo[which, rows, col * 128:(col + 1) * 128] = low

    prepare(core)
    wait_bytes(pbuf.at[0], pc_recv.at[0])
    prepare(1 - core)

    lane = lax.broadcasted_iota(jnp.int32, (64, 128), 1)

    def meridional(step):
        wait_bytes(zr.at[step], in_recv.at[step])
        v = [zr[step, :, s].reshape(64, 128) for s in range(8)]
        for k in range(3):
            bit = 1 << k
            low_half = (lane & bit) == 0
            new = list(v)
            for a in range(8):
                if a & bit:
                    continue
                b = a | bit
                new[a] = jnp.where(low_half, v[a], pltpu.roll(v[b], bit, 1))
                new[b] = jnp.where(low_half, pltpu.roll(v[a], 128 - bit, 1), v[b])
            v = new
        for j in range(8):
            for g in range(8):
                zct[g, pl.ds(j, 8, stride=8), :] = v[j][g * 8:(g + 1) * 8]
        high, low = split(jnp.concatenate([zct[g] for g in range(8)], axis=1))
        stacked = jnp.concatenate([high, low], axis=0)
        low_lanes = lax.broadcasted_iota(jnp.int32, (32, 128), 1) < 64
        for which in range(2):
            for col in range(2):
                cols = slice(col * 256, (col + 1) * 256)
                one = jnp.dot(stacked, p_hi[which, :, cols], preferred_element_type=F32)
                two = jnp.dot(high, p_lo[which, :, cols], preferred_element_type=F32)
                both = one[0:64] + one[64:128] + two
                for k in range(2):
                    t = which * 4 + col * 2 + k
                    a = both[0:32, k * 128:(k + 1) * 128]
                    b = both[32:64, k * 128:(k + 1) * 128]
                    even = jnp.where(low_lanes, a, pltpu.roll(b, 64, 1))
                    odd = jnp.where(low_lanes, pltpu.roll(a, 64, 1), b)
                    outs[step, 2 * t] = even.reshape(4, 8, 128)
                    outs[step, 2 * t + 1] = odd.reshape(4, 8, 128)

        pltpu.make_async_copy(
            outs.at[step, lat], gath.at[step, half, :, l8], out_recv.at[step]
        ).start()

        @pl.loop(1, 16)
        def _(j):
            to_lat = lax.rem(zz + j // 4, 4) * 4 + lax.rem(xx + lax.rem(j, 4), 4)
            pltpu.make_async_remote_copy(
                src_ref=outs.at[step, to_lat], dst_ref=gath.at[step, half, :, l8],
                send_sem=out_send.at[step], recv_sem=out_recv.at[step],
                device_id=(lon, to_lat, lev), device_id_type=MESH,
            ).start()

    for step in range(STEPS):
        meridional(step)

    def assemble(step):
        wait_bytes(gath.at[step], out_recv.at[step])
        for h2 in range(2):
            field = 3 * h2 + step
            for t in range(2):
                block = gath[step, h2, 2 * t:2 * t + 2].reshape(128, 128)
                turned = block.T
                for h in range(2):
                    sb = 2 * h + t
                    for n0 in range(0, 64, 8):
                        out_ref[pl.ds((n0 * 6 + field) * 4 + sb, 8, stride=24), :] = (
                            turned[h * 64 + n0:h * 64 + n0 + 8]
                        )

    for step in range(STEPS):
        assemble(step)

    for copy in halo_copies:
        copy.wait_send()
    for step in range(STEPS):
        wait_bytes(xs.at[pl.ds(0, 896)], lon_send.at[step])
        wait_in_sends(step)
        wait_bytes(outs.at[step, pl.ds(0, 15)], out_send.at[step])
    wait_bytes(pbuf.at[0, :, pl.ds(0, 192)], p_send.at[0])
    wait_bytes(pbuf.at[0, :, pl.ds(0, 768)], p_send.at[1])
    to_sibling.wait_send()


def on_device(fields_grid, hermite_proj):
    first_cat, twiddle, second_cat = tables()
    vmem = pl.BlockSpec(memory_space=pltpu.VMEM)
    dma = pltpu.SemaphoreType.DMA
    out = pl.pallas_call(
        kernel,
        out_shape=jax.ShapeDtypeStruct((1536, 128), F32),
        in_specs=[vmem] * 5,
        out_specs=vmem,
        scratch_shapes=[
            pltpu.VMEM((2, 64, 1024), F32),
            pltpu.VMEM((6 * 512, 128), F32),
            pltpu.VMEM((3, 8, 128, 128), F32),
            pltpu.VMEM((8, 128, 256), BF16),
            pltpu.VMEM((8, 128, 256), BF16),
            pltpu.VMEM((3, 8, 8, 8, 128), F32),
            pltpu.VMEM((3, 8, 8, 8, 128), F32),
            pltpu.VMEM((8, 64, 128), F32),
            pltpu.VMEM((2, 4, 1024, 128), F32),
            pltpu.VMEM((2, 1024, 512), BF16),
            pltpu.VMEM((2, 1024, 512), BF16),
            pltpu.VMEM((3, 16, 4, 8, 128), F32),
            pltpu.VMEM((3, 2, 4, 8, 8, 128), F32),
            dma((2,)), dma((2,)), dma((3,)), dma((3,)), dma((3,)), dma((3,)), dma((3,)), dma((3,)),
            dma((3,)), dma((4,)), dma((4, 4)), dma((2,)),
            pltpu.SemaphoreType.REGULAR,
        ],
        compiler_params=pltpu.CompilerParams(
            collective_id=0, has_side_effects=True, vmem_limit_bytes=48 * 1024 * 1024
        ),
    )(fields_grid, hermite_proj, first_cat, twiddle, second_cat)
    return out.reshape(64, 6, 1, 512)


def solution(mesh):
    in_specs = (P(None, "lev", "lat", "lon"), P("lat", None))
    out_specs = P("lat", None, "lev", "lon")
    return jax.shard_map(
        on_device, mesh=mesh, in_specs=in_specs, out_specs=out_specs, check_vma=False
    )
```

```python
import functools
import math

import jax
import jax.numpy as jnp
import ml_dtypes
import numpy as np
from jax import lax
from jax.experimental import pallas as pl
from jax.experimental.pallas import tpu as pltpu
from jax.sharding import PartitionSpec as P

MESH = pl.DeviceIdType.MESH
F32 = jnp.float32
BF16 = jnp.bfloat16
NLON = 8192
STEPS = 3


def split_np(table):
    high = table.astype(np.float32).astype(ml_dtypes.bfloat16)
    low = (table - high.astype(np.float64)).astype(np.float32).astype(ml_dtypes.bfloat16)
    return high, low


def tables():
    q = np.arange(64)
    p = np.arange(128)
    high_m = np.arange(32)
    first = 2.0 * np.pi * (np.outer(q, q) % 64) / 64
    first = np.concatenate([np.cos(first), -np.sin(first)], axis=0)
    f_high, f_low = split_np(first)
    first_cat = np.concatenate([f_high, f_low, f_high], axis=1)
    angle = 2.0 * np.pi * np.outer(q, p) / NLON
    twiddle = np.concatenate([np.cos(angle), np.sin(angle)], axis=0).astype(np.float32)
    second = 2.0 * np.pi * (np.outer(high_m, p) % 128) / 128
    cos_b, sin_b = np.cos(second), np.sin(second)
    second = np.concatenate(
        [np.concatenate([cos_b, sin_b], axis=1), np.concatenate([-sin_b, cos_b], axis=1)], axis=0
    ) / math.sqrt(NLON)
    s_high, s_low = split_np(second)
    second_cat = np.concatenate([s_high, s_low], axis=0)
    return first_cat, twiddle, second_cat


def split(value):
    high = value.astype(BF16)
    low = (value - high.astype(F32)).astype(BF16)
    return high, low


def wait_bytes(ref, sem):
    pltpu.make_async_copy(ref, ref, sem).wait()


def kernel(
    fields_hbm, herm_hbm, first_hbm, twiddle_hbm, second_hbm, out_ref,
    fields, first_ref, twiddle_ref, second_ref, halo, xs, xr, b_hi, b_lo, zs, zr, zct, pbuf, p_hi, p_lo, zb, outs, gath,
    halo_send, halo_recv, lon_send, lon_recv, in_send, in_recv, out_send, out_recv,
    p_send, pz_recv, px_recv, pc_recv, load, round_two,
):
    lon = lax.axis_index("lon")
    lat = lax.axis_index("lat")
    lev = lax.axis_index("lev")
    yy, core = lon // 2, lax.rem(lon, 2)
    zz, xx = lat // 4, lax.rem(lat, 4)
    half, l8 = lax.rem(lat, 2), lat // 2
    other = 1 - lev

    away = lax.rem(zz + 3 + 2 * lev, 4)
    partner_id = (lon, lat, other)
    away_id = (lon, away * 4 + xx, other)
    barrier = pltpu.get_barrier_semaphore()

    def greet(device_id):
        pl.semaphore_signal(barrier, inc=1, device_id=device_id, device_id_type=MESH)

    for off in range(1, 16):
        greet((lon, lax.rem(lat + off, 16), lev))
    greet(away_id)
    for off in range(1, 8):
        greet((lax.rem(lon + off, 8), lat, lev))
    for off in range(8):
        greet((lax.rem(lon + off, 8), lat, other))

    loads = [
        pltpu.make_async_copy(fields_hbm.at[f, 0], fields.at[f], load.at[f]) for f in (0, 5, 1, 3, 4)
    ]
    loads = dict(zip((0, 5, 1, 3, 4), loads))
    for copy in loads.values():
        copy.start()
    own_rows = pl.ds(pl.multiple_of(lat * 64, 64), 64)
    for col in range(4):
        lanes = pl.ds(pl.multiple_of(core * 512 + col * 128, 128), 128)
        pltpu.make_async_copy(herm_hbm.at[:, lanes], pbuf.at[core, col, own_rows], pc_recv.at[1]).start()
    constants = [
        pltpu.make_async_copy(hbm, ref, load.at[6 + n])
        for n, (hbm, ref) in enumerate(
            ((first_hbm, first_ref), (twiddle_hbm, twiddle_ref), (second_hbm, second_ref))
        )
    ]
    for copy in constants:
        copy.start()

    halo_copies = []
    for slot, field in enumerate((2, 4)):
        copy = pltpu.make_async_remote_copy(
            src_ref=fields_hbm.at[field, 0], dst_ref=halo.at[slot],
            send_sem=halo_send.at[slot], recv_sem=halo_recv.at[slot],
            device_id=partner_id, device_id_type=MESH,
        )
        halo_copies.append(copy)

    def make_products(dst_field, compute):
        @pl.loop(0, 8)
        def _(yb):
            rows = pl.ds(pl.multiple_of(yb * 8, 8), 8)
            value = compute(rows)
            for t in range(8):
                xs[pl.ds(dst_field * 512 + yb * 64 + t, 8, stride=8), :] = value[:, t * 128:(t + 1) * 128]

    def send_lon(step, to_core):
        field = 3 * to_core + step
        for dy in range(4):
            peer_y = lax.rem(yy + dy, 4)
            rows = pl.ds(pl.multiple_of(field * 512 + peer_y * 128, 128), 128)

            def remote():
                pltpu.make_async_remote_copy(
                    src_ref=xs.at[rows], dst_ref=xr.at[step, lon],
                    send_sem=lon_send.at[step], recv_sem=lon_recv.at[step],
                    device_id=(peer_y * 2 + to_core, lat, lev), device_id_type=MESH,
                ).start()

            if dy:
                remote()
            else:
                @pl.when(core != to_core)
                def _():
                    remote()

                @pl.when(core == to_core)
                def _():
                    pltpu.make_async_copy(xs.at[rows], xr.at[step, lon], lon_recv.at[step]).start()

    def wait_lon_sends(step):
        wait_bytes(xs.at[pl.ds(0, 896)], lon_send.at[step])

    beyond_id = (lon, away * 4 + xx, lev)
    quarter = pbuf.at[0, :, pl.ds(0, 64)]

    def rows_of(block_z, block_x, start=0, size=64):
        first = pl.multiple_of((block_z * 4 + block_x) * 64 + start, size)
        return pbuf.at[core, :, pl.ds(first, size)]

    def push(block, device_id, sem, slot):
        pltpu.make_async_remote_copy(
            src_ref=block, dst_ref=block, send_sem=p_send.at[slot], recv_sem=sem,
            device_id=device_id, device_id_type=MESH,
        ).start()

    right_id = (lon, zz * 4 + lax.rem(xx + 1, 4), lev)
    left_id = (lon, zz * 4 + lax.rem(xx + 3, 4), lev)

    def spread_x(slot, block_z):
        push(rows_of(block_z, xx), right_id, px_recv.at[slot, 0], 1)
        push(rows_of(block_z, xx), left_id, px_recv.at[slot, 1], 1)

    def relay_x(slot, block_z):
        left_x, right_x = lax.rem(xx + 3, 4), lax.rem(xx + 1, 4)
        wait_bytes(rows_of(block_z, left_x), px_recv.at[slot, 0])
        push(rows_of(block_z, left_x, 0, 32), right_id, px_recv.at[slot, 2], 3)
        wait_bytes(rows_of(block_z, right_x), px_recv.at[slot, 1])
        push(rows_of(block_z, right_x, 32, 32), left_id, px_recv.at[slot, 3], 3)

    toward = lax.rem(zz + 5 - 2 * lev, 4)
    far = lax.rem(zz + 2, 4)
    blocks = (zz, away, toward, far)

    def zonal(step):
        wait_bytes(xr.at[step], lon_recv.at[step])
        if step == 0:
            for copy in constants:
                copy.wait()
        cos_t, sin_t = twiddle_ref[0:64, :], twiddle_ref[64:128, :]

        for u in range(8):
            cats = []
            for k in range(2):
                block = xr[step, :, pl.ds(u * 16 + k * 8, 8), :].reshape(64, 128)
                high, low = split(block)
                cats.append(jnp.concatenate([high, high, low], axis=0))
            cat = jnp.concatenate(cats, axis=1)
            first = jnp.dot(first_ref[...], cat, preferred_element_type=F32)
            res, ims = [], []
            for k in range(2):
                re = first[0:64, k * 128:(k + 1) * 128]
                im = first[64:128, k * 128:(k + 1) * 128]
                res.append((re * cos_t + im * sin_t).reshape(8, 8, 128))
                ims.append((im * cos_t - re * sin_t).reshape(8, 8, 128))
            rows = pl.ds(u * 16, 16)
            for part, pair in enumerate((res, ims)):
                high, low = split(jnp.concatenate(pair, axis=1))
                b_hi[:, rows, part * 128:(part + 1) * 128] = high
                b_lo[:, rows, part * 128:(part + 1) * 128] = low

        for u in range(4):
            pair = pl.ds(u * 2, 2)
            high = b_hi[pair].reshape(256, 256)
            low = b_lo[pair].reshape(256, 256)
            nt = (((1,), (1,)), ((), ()))
            one = lax.dot_general(second_ref[...], high, nt, preferred_element_type=F32)
            two = lax.dot_general(second_ref[0:64, :], low, nt, preferred_element_type=F32)
            both = one[0:64] + one[64:128] + two
            for k in range(2):
                zs[step, :, u * 2 + k] = both[:, k * 128:(k + 1) * 128].reshape(8, 8, 128)

    source = lat * 4 + yy
    my_g, my_s = source // 8, lax.rem(source, 8)

    to_x = [lax.rem(xx + 2 * dx, 4) // 2 * 2 + core for dx in range(2)]
    to_lats = {(dz, dx): lax.rem(zz + dz, 4) * 4 + to_x[dx] for dz in range(4) for dx in range(2)}
    to_l8 = {key: value // 2 for key, value in to_lats.items()}
    crossed = jnp.where(core == 1, other, lev)

    def send_in(step):
        to_lev = crossed if step else lev

        @pl.loop(0, 8)
        def _(k):
            to_lon = lax.rem(lon + k, 8)
            for dz in (2, 1, 3, 0):
                for dx in range(2):
                    to_lat = to_lats[dz, dx]
                    src = zs.at[step, to_lon, to_l8[dz, dx]]
                    dst = zr.at[step, my_g, my_s]

                    def remote():
                        pltpu.make_async_remote_copy(
                            src_ref=src, dst_ref=dst,
                            send_sem=in_send.at[step], recv_sem=in_recv.at[step],
                            device_id=(to_lon, to_lat, to_lev), device_id_type=MESH,
                        ).start()

                    if dz or dx:
                        remote()
                        continue
                    mine = jnp.logical_and(
                        jnp.logical_and(k == 0, to_lat == lat), to_lev == lev
                    )

                    @pl.when(jnp.logical_not(mine))
                    def _():
                        remote()

                    @pl.when(mine)
                    def _():
                        pltpu.make_async_copy(src, dst, in_recv.at[step]).start()

    def wait_in_sends(step):
        flip = jnp.logical_and(core == 1, step >= 1)
        has_self = jnp.logical_and(half == core, jnp.logical_not(flip))

        @pl.when(has_self)
        def _():
            wait_bytes(zs.at[step, pl.ds(0, 7)], in_send.at[step])
            wait_bytes(zs.at[step, 0, pl.ds(0, 7)], in_send.at[step])

        @pl.when(jnp.logical_not(has_self))
        def _():
            wait_bytes(zs.at[step], in_send.at[step])

    def send_round_two():
        for off in range(1, 16):
            pl.semaphore_signal(
                round_two, inc=1, device_id=(lon, lax.rem(lat + off, 16), lev), device_id_type=MESH
            )

    loads[0].wait()
    loads[5].wait()
    make_products(0, lambda r: fields[0, r, :] * fields[5, r, :])
    loads[1].wait()
    loads[3].wait()
    make_products(3, lambda r: fields[1, r, :] * fields[3, r, :])
    pl.semaphore_wait(barrier, 31)
    for copy in halo_copies:
        copy.start()
    send_lon(0, 0)
    send_lon(0, 1)
    send_round_two()
    wait_bytes(quarter, pc_recv.at[1])
    push(rows_of(zz, xx), away_id, pz_recv.at[0], 0)
    push(rows_of(zz, xx), beyond_id, pz_recv.at[1], 0)
    spread_x(0, zz)
    make_products(1, lambda r: fields[0, r, :] * fields[1, r, :])
    loads[4].wait()
    make_products(2, lambda r: fields[0, r, :] * fields[4, r, :])
    sign = jnp.where(lev == 0, F32(-0.5), F32(0.5))
    halo_copies[0].wait_recv()
    make_products(4, lambda r: halo[0, r, :] * (fields[0, r, :] * sign))
    wait_bytes(quarter, pz_recv.at[1])
    push(rows_of(toward, xx), away_id, pz_recv.at[2], 0)
    spread_x(2, toward)
    wait_bytes(quarter, pz_recv.at[0])
    spread_x(1, away)
    relay_x(0, blocks[0])
    wait_lon_sends(0)
    send_lon(1, 0)
    send_lon(1, 1)
    zonal(0)
    pl.semaphore_wait(round_two, 15)
    send_in(0)
    halo_copies[1].wait_recv()
    make_products(
        5,
        lambda r: halo[0, r, :] * (fields[3, r, :] * sign)
        - 0.25 * (fields[4, r, :] - 2.0 * halo[1, r, :]),
    )
    wait_lon_sends(1)
    send_lon(2, 0)
    send_lon(2, 1)
    wait_bytes(quarter, pz_recv.at[2])
    spread_x(3, far)
    relay_x(2, blocks[2])
    relay_x(1, blocks[1])
    zonal(1)
    send_in(1)
    relay_x(3, blocks[3])
    zonal(2)
    send_in(2)

    for slot in range(4):
        for side in range(2):
            wait_bytes(pbuf.at[0, :, pl.ds(0, 32)], px_recv.at[slot, 2 + side])
    to_sibling = pltpu.make_async_remote_copy(
        src_ref=pbuf.at[core], dst_ref=pbuf.at[core],
        send_sem=p_send.at[2], recv_sem=pc_recv.at[0],
        device_id=(lon + 1 - 2 * core, lat, lev), device_id_type=MESH,
    )
    to_sibling.start()

    def prepare(which):
        @pl.loop(0, 8)
        def _(g):
          for u in range(8):
            for col in range(4):
                pieces = [
                    pbuf[which, col, pl.ds(g * 128 + u * 2 + k, 8, stride=16), :]
                    for k in range(2)
                ]
                high, low = split(jnp.concatenate(pieces, axis=0))
                rows = pl.ds(pl.multiple_of(g * 128 + u * 16, 16), 16)
                p_hi[which, rows, col * 128:(col + 1) * 128] = high
                p_lo[which, rows, col * 128:(col + 1) * 128] = low

    lane = lax.broadcasted_iota(jnp.int32, (64, 128), 1)
    low_lanes = lax.broadcasted_iota(jnp.int32, (32, 128), 1) < 64

    def transpose_in(step):
        wait_bytes(zr.at[step], in_recv.at[step])
        v = [zr[step, :, s].reshape(64, 128) for s in range(8)]
        for k in range(3):
            bit = 1 << k
            low_half = (lane & bit) == 0
            new = list(v)
            for a in range(8):
                if a & bit:
                    continue
                b = a | bit
                new[a] = jnp.where(low_half, v[a], pltpu.roll(v[b], bit, 1))
                new[b] = jnp.where(low_half, pltpu.roll(v[a], 128 - bit, 1), v[b])
            v = new
        for j in range(8):
            for g in range(8):
                zct[g, pl.ds(j, 8, stride=8), :] = v[j][g * 8:(g + 1) * 8]
        high, low = split(jnp.concatenate([zct[g] for g in range(8)], axis=1))
        zb[0:64, :] = high
        zb[64:128, :] = low

    def project(step, which):
        for col in range(2):
            cols = slice(col * 256, (col + 1) * 256)
            one = jnp.dot(zb[...], p_hi[which, :, cols], preferred_element_type=F32)
            two = jnp.dot(zb[0:64, :], p_lo[which, :, cols], preferred_element_type=F32)
            both = one[0:64] + one[64:128] + two
            for k in range(2):
                t = which * 4 + col * 2 + k
                a = both[0:32, k * 128:(k + 1) * 128]
                b = both[32:64, k * 128:(k + 1) * 128]
                even = jnp.where(low_lanes, a, pltpu.roll(b, 64, 1))
                odd = jnp.where(low_lanes, pltpu.roll(a, 64, 1), b)
                outs[step, 2 * t] = even.reshape(4, 8, 128)
                outs[step, 2 * t + 1] = odd.reshape(4, 8, 128)

        for j in range(8):
            to_lat = which * 8 + lax.rem(lat + 4 + j, 8)

            @pl.when(to_lat != lat)
            def _():
                pltpu.make_async_remote_copy(
                    src_ref=outs.at[step, to_lat], dst_ref=gath.at[step, half, :, l8],
                    send_sem=out_send.at[step], recv_sem=out_recv.at[step],
                    device_id=(lon, to_lat, lev), device_id_type=MESH,
                ).start()

            @pl.when(to_lat == lat)
            def _():
                pltpu.make_async_copy(
                    outs.at[step, to_lat], gath.at[step, half, :, l8], out_recv.at[step]
                ).start()

    prepare(core)
    transpose_in(0)
    project(0, core)
    wait_bytes(pbuf.at[0], pc_recv.at[0])
    prepare(1 - core)
    project(0, 1 - core)
    transpose_in(1)
    project(1, core)
    project(1, 1 - core)
    transpose_in(2)
    project(2, core)
    project(2, 1 - core)

    def assemble(step):
        wait_bytes(gath.at[step], out_recv.at[step])
        for h2 in range(2):
            field = 3 * h2 + step
            for t in range(2):
                block = gath[step, h2, 2 * t:2 * t + 2].reshape(128, 128)
                turned = block.T
                for h in range(2):
                    sb = 2 * h + t
                    for n0 in range(0, 64, 8):
                        out_ref[pl.ds((n0 * 6 + field) * 4 + sb, 8, stride=24), :] = (
                            turned[h * 64 + n0:h * 64 + n0 + 8]
                        )

    for step in range(STEPS):
        assemble(step)

    wait_lon_sends(2)
    for copy in halo_copies:
        copy.wait_send()
    for step in range(STEPS):
        wait_in_sends(step)
        wait_bytes(outs.at[step, pl.ds(0, 15)], out_send.at[step])
    wait_bytes(pbuf.at[0, :, pl.ds(0, 192)], p_send.at[0])
    wait_bytes(pbuf.at[0, :, pl.ds(0, 512)], p_send.at[1])
    wait_bytes(pbuf.at[0, :, pl.ds(0, 256)], p_send.at[3])
    to_sibling.wait_send()


def on_device(fields_grid, hermite_proj):
    first_cat, twiddle, second_cat = tables()
    vmem = pl.BlockSpec(memory_space=pltpu.VMEM)
    dma = pltpu.SemaphoreType.DMA
    out = pl.pallas_call(
        kernel,
        out_shape=jax.ShapeDtypeStruct((1536, 128), F32),
        in_specs=[pl.BlockSpec(memory_space=pltpu.HBM)] * 5,
        out_specs=vmem,
        scratch_shapes=[
            pltpu.VMEM((6, 64, 1024), F32),
            pltpu.VMEM((128, 192), BF16),
            pltpu.VMEM((128, 128), F32),
            pltpu.VMEM((128, 256), BF16),
            pltpu.VMEM((2, 64, 1024), F32),
            pltpu.VMEM((6 * 512, 128), F32),
            pltpu.VMEM((3, 8, 128, 128), F32),
            pltpu.VMEM((8, 128, 256), BF16),
            pltpu.VMEM((8, 128, 256), BF16),
            pltpu.VMEM((3, 8, 8, 8, 128), F32),
            pltpu.VMEM((3, 8, 8, 8, 128), F32),
            pltpu.VMEM((8, 64, 128), F32),
            pltpu.VMEM((2, 4, 1024, 128), F32),
            pltpu.VMEM((2, 1024, 512), BF16),
            pltpu.VMEM((2, 1024, 512), BF16),
            pltpu.VMEM((128, 1024), BF16),
            pltpu.VMEM((3, 16, 4, 8, 128), F32),
            pltpu.VMEM((3, 2, 4, 8, 8, 128), F32),
            dma((2,)), dma((2,)), dma((3,)), dma((3,)), dma((3,)), dma((3,)), dma((3,)), dma((3,)),
            dma((4,)), dma((3,)), dma((4, 4)), dma((2,)), dma((9,)),
            pltpu.SemaphoreType.REGULAR,
        ],
        compiler_params=pltpu.CompilerParams(
            collective_id=0, has_side_effects=True, vmem_limit_bytes=60 * 1024 * 1024
        ),
    )(fields_grid, hermite_proj, first_cat, twiddle, second_cat)
    return out.reshape(64, 6, 1, 512)


def solution(mesh):
    in_specs = (P(None, "lev", "lat", "lon"), P("lat", None))
    out_specs = P("lat", None, "lev", "lon")
    return jax.shard_map(
        on_device, mesh=mesh, in_specs=in_specs, out_specs=out_specs, check_vma=False
    )
```

```python
import functools
import math

import jax
import jax.numpy as jnp
import ml_dtypes
import numpy as np
from jax import lax
from jax.experimental import pallas as pl
from jax.experimental.pallas import tpu as pltpu
from jax.sharding import PartitionSpec as P

MESH = pl.DeviceIdType.MESH
F32 = jnp.float32
BF16 = jnp.bfloat16
NLON = 8192
STEPS = 3


def split_np(table):
    high = table.astype(np.float32).astype(ml_dtypes.bfloat16)
    low = (table - high.astype(np.float64)).astype(np.float32).astype(ml_dtypes.bfloat16)
    return high, low


def tables():
    q = np.arange(64)
    p = np.arange(128)
    high_m = np.arange(32)
    first = 2.0 * np.pi * (np.outer(q, q) % 64) / 64
    first = np.concatenate([np.cos(first), -np.sin(first)], axis=0)
    f_high, f_low = split_np(first)
    first_cat = np.concatenate([f_high, f_low, f_high], axis=1)
    angle = 2.0 * np.pi * np.outer(q, p) / NLON
    twiddle = np.concatenate([np.cos(angle), np.sin(angle)], axis=0).astype(np.float32)
    second = 2.0 * np.pi * (np.outer(high_m, p) % 128) / 128
    cos_b, sin_b = np.cos(second), np.sin(second)
    second = np.concatenate(
        [np.concatenate([cos_b, sin_b], axis=1), np.concatenate([-sin_b, cos_b], axis=1)], axis=0
    ) / math.sqrt(NLON)
    s_high, s_low = split_np(second)
    second_cat = np.concatenate([s_high, s_low], axis=0)
    return first_cat, twiddle, second_cat


def split(value):
    high = value.astype(BF16)
    low = (value - high.astype(F32)).astype(BF16)
    return high, low


def wait_bytes(ref, sem):
    pltpu.make_async_copy(ref, ref, sem).wait()


def kernel(
    fields_hbm, herm_hbm, first_hbm, twiddle_hbm, second_hbm, gath,
    fields, first_ref, twiddle_ref, second_ref, halo, xs, xr, b_hi, b_lo, zs, zr, zct, pbuf, p_hi, p_lo, zb, outs,
    halo_send, halo_recv, lon_send, lon_recv, in_send, in_recv, out_send, out_recv,
    p_send, pz_recv, px_recv, pc_recv, load, round_two,
):
    lon = lax.axis_index("lon")
    lat = lax.axis_index("lat")
    lev = lax.axis_index("lev")
    yy, core = lon // 2, lax.rem(lon, 2)
    zz, xx = lat // 4, lax.rem(lat, 4)
    half, l8 = lax.rem(lat, 2), lat // 2
    other = 1 - lev

    loads = [
        pltpu.make_async_copy(fields_hbm.at[f, 0], fields.at[f], load.at[f]) for f in (0, 5, 1, 3, 4)
    ]
    loads = dict(zip((0, 5, 1, 3, 4), loads))
    for copy in loads.values():
        copy.start()
    own_rows = pl.ds(pl.multiple_of(lat * 64, 64), 64)
    for col in range(4):
        lanes = pl.ds(pl.multiple_of(core * 512 + col * 128, 128), 128)
        pltpu.make_async_copy(herm_hbm.at[:, lanes], pbuf.at[core, col, own_rows], pc_recv.at[1]).start()
    constants = [
        pltpu.make_async_copy(hbm, ref, load.at[6 + n])
        for n, (hbm, ref) in enumerate(
            ((first_hbm, first_ref), (twiddle_hbm, twiddle_ref), (second_hbm, second_ref))
        )
    ]
    for copy in constants:
        copy.start()

    away = lax.rem(zz + 3 + 2 * lev, 4)
    partner_id = (lon, lat, other)
    away_id = (lon, away * 4 + xx, other)
    barrier = pltpu.get_barrier_semaphore()

    def greet(device_id):
        pl.semaphore_signal(barrier, inc=1, device_id=device_id, device_id_type=MESH)

    for off in range(1, 16):
        greet((lon, lax.rem(lat + off, 16), lev))
    greet(away_id)
    for off in range(1, 8):
        greet((lax.rem(lon + off, 8), lat, lev))
    for off in range(8):
        greet((lax.rem(lon + off, 8), lat, other))

    halo_copies = []
    for slot, field in enumerate((2, 4)):
        copy = pltpu.make_async_remote_copy(
            src_ref=fields_hbm.at[field, 0], dst_ref=halo.at[slot],
            send_sem=halo_send.at[slot], recv_sem=halo_recv.at[slot],
            device_id=partner_id, device_id_type=MESH,
        )
        halo_copies.append(copy)

    def make_products(dst_field, compute):
        @pl.loop(0, 8)
        def _(yb):
            rows = pl.ds(pl.multiple_of(yb * 8, 8), 8)
            value = compute(rows)
            for t in range(8):
                xs[pl.ds(dst_field * 512 + yb * 64 + t, 8, stride=8), :] = value[:, t * 128:(t + 1) * 128]

    def send_lon(step, to_core):
        field = 3 * to_core + step
        for dy in range(4):
            peer_y = lax.rem(yy + dy, 4)
            rows = pl.ds(pl.multiple_of(field * 512 + peer_y * 128, 128), 128)

            def remote():
                pltpu.make_async_remote_copy(
                    src_ref=xs.at[rows], dst_ref=xr.at[step, lon],
                    send_sem=lon_send.at[step], recv_sem=lon_recv.at[step],
                    device_id=(peer_y * 2 + to_core, lat, lev), device_id_type=MESH,
                ).start()

            if dy:
                remote()
            else:
                @pl.when(core != to_core)
                def _():
                    remote()

                @pl.when(core == to_core)
                def _():
                    pltpu.make_async_copy(xs.at[rows], xr.at[step, lon], lon_recv.at[step]).start()

    def wait_lon_sends(step):
        wait_bytes(xs.at[pl.ds(0, 896)], lon_send.at[step])

    beyond_id = (lon, away * 4 + xx, lev)
    quarter = pbuf.at[0, :, pl.ds(0, 64)]

    def rows_of(block_z, block_x, start=0, size=64):
        first = pl.multiple_of((block_z * 4 + block_x) * 64 + start, size)
        return pbuf.at[core, :, pl.ds(first, size)]

    def push(block, device_id, sem, slot):
        pltpu.make_async_remote_copy(
            src_ref=block, dst_ref=block, send_sem=p_send.at[slot], recv_sem=sem,
            device_id=device_id, device_id_type=MESH,
        ).start()

    right_id = (lon, zz * 4 + lax.rem(xx + 1, 4), lev)
    left_id = (lon, zz * 4 + lax.rem(xx + 3, 4), lev)

    def spread_x(slot, block_z):
        push(rows_of(block_z, xx), right_id, px_recv.at[slot, 0], 1)
        push(rows_of(block_z, xx), left_id, px_recv.at[slot, 1], 1)

    def relay_x(slot, block_z):
        left_x, right_x = lax.rem(xx + 3, 4), lax.rem(xx + 1, 4)
        wait_bytes(rows_of(block_z, left_x), px_recv.at[slot, 0])
        push(rows_of(block_z, left_x, 0, 32), right_id, px_recv.at[slot, 2], 3)
        wait_bytes(rows_of(block_z, right_x), px_recv.at[slot, 1])
        push(rows_of(block_z, right_x, 32, 32), left_id, px_recv.at[slot, 3], 3)

    toward = lax.rem(zz + 5 - 2 * lev, 4)
    far = lax.rem(zz + 2, 4)
    blocks = (zz, away, toward, far)

    def zonal(step):
        wait_bytes(xr.at[step], lon_recv.at[step])
        if step == 0:
            for copy in constants:
                copy.wait()
        cos_t, sin_t = twiddle_ref[0:64, :], twiddle_ref[64:128, :]

        for u in range(8):
            cats = []
            for k in range(2):
                block = xr[step, :, pl.ds(u * 16 + k * 8, 8), :].reshape(64, 128)
                high, low = split(block)
                cats.append(jnp.concatenate([high, high, low], axis=0))
            cat = jnp.concatenate(cats, axis=1)
            first = jnp.dot(first_ref[...], cat, preferred_element_type=F32)
            res, ims = [], []
            for k in range(2):
                re = first[0:64, k * 128:(k + 1) * 128]
                im = first[64:128, k * 128:(k + 1) * 128]
                res.append((re * cos_t + im * sin_t).reshape(8, 8, 128))
                ims.append((im * cos_t - re * sin_t).reshape(8, 8, 128))
            rows = pl.ds(u * 16, 16)
            for part, pair in enumerate((res, ims)):
                high, low = split(jnp.concatenate(pair, axis=1))
                b_hi[:, rows, part * 128:(part + 1) * 128] = high
                b_lo[:, rows, part * 128:(part + 1) * 128] = low

        for u in range(4):
            pair = pl.ds(u * 2, 2)
            high = b_hi[pair].reshape(256, 256)
            low = b_lo[pair].reshape(256, 256)
            nt = (((1,), (1,)), ((), ()))
            one = lax.dot_general(second_ref[...], high, nt, preferred_element_type=F32)
            two = lax.dot_general(second_ref[0:64, :], low, nt, preferred_element_type=F32)
            both = one[0:64] + one[64:128] + two
            for k in range(2):
                zs[step, :, u * 2 + k] = both[:, k * 128:(k + 1) * 128].reshape(8, 8, 128)

    source = lat * 4 + yy
    my_g, my_s = source // 8, lax.rem(source, 8)

    to_x = [lax.rem(xx + 2 * dx, 4) // 2 * 2 + core for dx in range(2)]
    to_lats = {(dz, dx): lax.rem(zz + dz, 4) * 4 + to_x[dx] for dz in range(4) for dx in range(2)}
    to_l8 = {key: value // 2 for key, value in to_lats.items()}
    crossed = jnp.where(core == 1, other, lev)

    def send_in(step):
        to_lev = crossed if step else lev

        @pl.loop(0, 8)
        def _(k):
            to_lon = lax.rem(lon + k, 8)
            for dz in (2, 1, 3, 0):
                for dx in range(2):
                    to_lat = to_lats[dz, dx]
                    src = zs.at[step, to_lon, to_l8[dz, dx]]
                    dst = zr.at[step, my_g, my_s]

                    def remote():
                        pltpu.make_async_remote_copy(
                            src_ref=src, dst_ref=dst,
                            send_sem=in_send.at[step], recv_sem=in_recv.at[step],
                            device_id=(to_lon, to_lat, to_lev), device_id_type=MESH,
                        ).start()

                    if dz or dx:
                        remote()
                        continue
                    mine = jnp.logical_and(
                        jnp.logical_and(k == 0, to_lat == lat), to_lev == lev
                    )

                    @pl.when(jnp.logical_not(mine))
                    def _():
                        remote()

                    @pl.when(mine)
                    def _():
                        pltpu.make_async_copy(src, dst, in_recv.at[step]).start()

    def wait_in_sends(step):
        flip = jnp.logical_and(core == 1, step >= 1)
        has_self = jnp.logical_and(half == core, jnp.logical_not(flip))

        @pl.when(has_self)
        def _():
            wait_bytes(zs.at[step, pl.ds(0, 7)], in_send.at[step])
            wait_bytes(zs.at[step, 0, pl.ds(0, 7)], in_send.at[step])

        @pl.when(jnp.logical_not(has_self))
        def _():
            wait_bytes(zs.at[step], in_send.at[step])

    def send_round_two():
        for off in range(1, 16):
            pl.semaphore_signal(
                round_two, inc=1, device_id=(lon, lax.rem(lat + off, 16), lev), device_id_type=MESH
            )

    loads[0].wait()
    loads[5].wait()
    make_products(0, lambda r: fields[0, r, :] * fields[5, r, :])
    loads[1].wait()
    loads[3].wait()
    make_products(3, lambda r: fields[1, r, :] * fields[3, r, :])
    pl.semaphore_wait(barrier, 31)
    for copy in halo_copies:
        copy.start()
    send_lon(0, 0)
    send_lon(0, 1)
    send_round_two()
    wait_bytes(quarter, pc_recv.at[1])
    push(rows_of(zz, xx), away_id, pz_recv.at[0], 0)
    push(rows_of(zz, xx), beyond_id, pz_recv.at[1], 0)
    spread_x(0, zz)
    make_products(1, lambda r: fields[0, r, :] * fields[1, r, :])
    loads[4].wait()
    make_products(2, lambda r: fields[0, r, :] * fields[4, r, :])
    sign = jnp.where(lev == 0, F32(-0.5), F32(0.5))
    send_lon(1, 0)
    wait_bytes(quarter, pz_recv.at[1])
    push(rows_of(toward, xx), away_id, pz_recv.at[2], 0)
    spread_x(2, toward)
    wait_bytes(quarter, pz_recv.at[0])
    spread_x(1, away)
    halo_copies[0].wait_recv()
    make_products(4, lambda r: halo[0, r, :] * (fields[0, r, :] * sign))
    send_lon(1, 1)
    zonal(0)
    pl.semaphore_wait(round_two, 15)
    send_in(0)
    relay_x(0, blocks[0])
    halo_copies[1].wait_recv()
    make_products(
        5,
        lambda r: halo[0, r, :] * (fields[3, r, :] * sign)
        - 0.25 * (fields[4, r, :] - 2.0 * halo[1, r, :]),
    )
    wait_lon_sends(1)
    send_lon(2, 0)
    send_lon(2, 1)
    wait_bytes(quarter, pz_recv.at[2])
    spread_x(3, far)
    relay_x(2, blocks[2])
    relay_x(1, blocks[1])
    zonal(1)
    send_in(1)
    relay_x(3, blocks[3])
    zonal(2)
    send_in(2)

    for slot in range(4):
        for side in range(2):
            wait_bytes(pbuf.at[0, :, pl.ds(0, 32)], px_recv.at[slot, 2 + side])
    to_sibling = pltpu.make_async_remote_copy(
        src_ref=pbuf.at[core], dst_ref=pbuf.at[core],
        send_sem=p_send.at[2], recv_sem=pc_recv.at[0],
        device_id=(lon + 1 - 2 * core, lat, lev), device_id_type=MESH,
    )
    to_sibling.start()

    def prepare(which):
        @pl.loop(0, 8)
        def _(g):
          for u in range(8):
            for col in range(4):
                pieces = [
                    pbuf[which, col, pl.ds(g * 128 + u * 2 + k, 8, stride=16), :]
                    for k in range(2)
                ]
                high, low = split(jnp.concatenate(pieces, axis=0))
                rows = pl.ds(pl.multiple_of(g * 128 + u * 16, 16), 16)
                p_hi[which, rows, col * 128:(col + 1) * 128] = high
                p_lo[which, rows, col * 128:(col + 1) * 128] = low

    lane = lax.broadcasted_iota(jnp.int32, (64, 128), 1)
    low_lanes = lax.broadcasted_iota(jnp.int32, (32, 128), 1) < 64

    def transpose_in(step):
        wait_bytes(zr.at[step], in_recv.at[step])
        v = [zr[step, :, s].reshape(64, 128) for s in range(8)]
        for k in range(3):
            bit = 1 << k
            low_half = (lane & bit) == 0
            new = list(v)
            for a in range(8):
                if a & bit:
                    continue
                b = a | bit
                new[a] = jnp.where(low_half, v[a], pltpu.roll(v[b], bit, 1))
                new[b] = jnp.where(low_half, pltpu.roll(v[a], 128 - bit, 1), v[b])
            v = new
        for j in range(8):
            for g in range(8):
                zct[g, pl.ds(j, 8, stride=8), :] = v[j][g * 8:(g + 1) * 8]
        high, low = split(jnp.concatenate([zct[g] for g in range(8)], axis=1))
        zb[0:64, :] = high
        zb[64:128, :] = low

    def project(step, which):
        for col in range(2):
            cols = slice(col * 256, (col + 1) * 256)
            one = jnp.dot(zb[...], p_hi[which, :, cols], preferred_element_type=F32)
            two = jnp.dot(zb[0:64, :], p_lo[which, :, cols], preferred_element_type=F32)
            both = one[0:64] + one[64:128] + two
            for k in range(2):
                t = which * 4 + col * 2 + k
                a = both[0:32, k * 128:(k + 1) * 128]
                b = both[32:64, k * 128:(k + 1) * 128]
                even = jnp.where(low_lanes, a, pltpu.roll(b, 64, 1))
                odd = jnp.where(low_lanes, pltpu.roll(a, 64, 1), b)
                outs[step, 2 * t] = even.reshape(4, 8, 128)
                outs[step, 2 * t + 1] = odd.reshape(4, 8, 128)

        for j in range(8):
            to_lat = which * 8 + lax.rem(lat + 4 + j, 8)

            @pl.when(to_lat != lat)
            def _():
                pltpu.make_async_remote_copy(
                    src_ref=outs.at[step, to_lat], dst_ref=gath.at[step, half, :, l8],
                    send_sem=out_send.at[step], recv_sem=out_recv.at[step],
                    device_id=(lon, to_lat, lev), device_id_type=MESH,
                ).start()

            @pl.when(to_lat == lat)
            def _():
                pltpu.make_async_copy(
                    outs.at[step, to_lat], gath.at[step, half, :, l8], out_recv.at[step]
                ).start()

    prepare(core)
    transpose_in(0)
    project(0, core)
    wait_bytes(pbuf.at[0], pc_recv.at[0])
    prepare(1 - core)
    project(0, 1 - core)
    transpose_in(1)
    project(1, core)
    project(1, 1 - core)
    transpose_in(2)
    project(2, core)
    project(2, 1 - core)

    for step in range(STEPS):
        wait_bytes(gath.at[step], out_recv.at[step])

    wait_lon_sends(2)
    wait_lon_sends(0)
    for copy in halo_copies:
        copy.wait_send()
    for step in range(STEPS):
        wait_in_sends(step)
        wait_bytes(outs.at[step, pl.ds(0, 15)], out_send.at[step])
    wait_bytes(pbuf.at[0, :, pl.ds(0, 192)], p_send.at[0])
    wait_bytes(pbuf.at[0, :, pl.ds(0, 512)], p_send.at[1])
    wait_bytes(pbuf.at[0, :, pl.ds(0, 256)], p_send.at[3])
    to_sibling.wait_send()


def assemble(gath_hbm, out_ref, gath, load):
    copies = [
        pltpu.make_async_copy(gath_hbm.at[step], gath.at[step], load.at[step]) for step in range(STEPS)
    ]
    for copy in copies:
        copy.start()
    for step in range(STEPS):
        copies[step].wait()
        for half in range(2):
            field = 3 * half + step
            for t in range(2):
                turned = gath[step, half, 2 * t:2 * t + 2].reshape(128, 128).T
                for h in range(2):
                    sb = 2 * h + t
                    for n0 in range(0, 64, 8):
                        out_ref[pl.ds((n0 * 6 + field) * 4 + sb, 8, stride=24), :] = (
                            turned[h * 64 + n0:h * 64 + n0 + 8]
                        )


def on_device(fields_grid, hermite_proj):
    first_cat, twiddle, second_cat = tables()
    hbm = pl.BlockSpec(memory_space=pltpu.HBM)
    dma = pltpu.SemaphoreType.DMA
    gathered = pl.pallas_call(
        kernel,
        out_shape=jax.ShapeDtypeStruct((3, 2, 4, 8, 8, 128), F32),
        in_specs=[hbm] * 5,
        out_specs=hbm,
        scratch_shapes=[
            pltpu.VMEM((6, 64, 1024), F32),
            pltpu.VMEM((128, 192), BF16),
            pltpu.VMEM((128, 128), F32),
            pltpu.VMEM((128, 256), BF16),
            pltpu.VMEM((2, 64, 1024), F32),
            pltpu.VMEM((6 * 512, 128), F32),
            pltpu.VMEM((3, 8, 128, 128), F32),
            pltpu.VMEM((8, 128, 256), BF16),
            pltpu.VMEM((8, 128, 256), BF16),
            pltpu.VMEM((3, 8, 8, 8, 128), F32),
            pltpu.VMEM((3, 8, 8, 8, 128), F32),
            pltpu.VMEM((8, 64, 128), F32),
            pltpu.VMEM((2, 4, 1024, 128), F32),
            pltpu.VMEM((2, 1024, 512), BF16),
            pltpu.VMEM((2, 1024, 512), BF16),
            pltpu.VMEM((128, 1024), BF16),
            pltpu.VMEM((3, 16, 4, 8, 128), F32),
            dma((2,)), dma((2,)), dma((3,)), dma((3,)), dma((3,)), dma((3,)), dma((3,)), dma((3,)),
            dma((4,)), dma((3,)), dma((4, 4)), dma((2,)), dma((9,)),
            pltpu.SemaphoreType.REGULAR,
        ],
        compiler_params=pltpu.CompilerParams(
            collective_id=0, has_side_effects=True, vmem_limit_bytes=60 * 1024 * 1024
        ),
    )(fields_grid, hermite_proj, first_cat, twiddle, second_cat)
    out = pl.pallas_call(
        assemble,
        out_shape=jax.ShapeDtypeStruct((1536, 128), F32),
        in_specs=[hbm],
        out_specs=pl.BlockSpec(memory_space=pltpu.VMEM),
        scratch_shapes=[pltpu.VMEM((3, 2, 4, 8, 8, 128), F32), dma((3,))],
        compiler_params=pltpu.CompilerParams(vmem_limit_bytes=60 * 1024 * 1024),
    )(gathered)
    return out.reshape(64, 6, 1, 512)


def solution(mesh):
    in_specs = (P(None, "lev", "lat", "lon"), P("lat", None))
    out_specs = P("lat", None, "lev", "lon")
    return jax.shard_map(
        on_device, mesh=mesh, in_specs=in_specs, out_specs=out_specs, check_vma=False
    )
```

```python
import functools
import math

import jax
import jax.numpy as jnp
import ml_dtypes
import numpy as np
from jax import lax
from jax.experimental import pallas as pl
from jax.experimental.pallas import tpu as pltpu
from jax.sharding import PartitionSpec as P

MESH = pl.DeviceIdType.MESH
F32 = jnp.float32
BF16 = jnp.bfloat16
NLON = 8192
STEPS = 3


def split_np(table):
    high = table.astype(np.float32).astype(ml_dtypes.bfloat16)
    low = (table - high.astype(np.float64)).astype(np.float32).astype(ml_dtypes.bfloat16)
    return high, low


def tables():
    q = np.arange(64)
    p = np.arange(128)
    high_m = np.arange(32)
    first = 2.0 * np.pi * (np.outer(q, q) % 64) / 64
    first = np.concatenate([np.cos(first), -np.sin(first)], axis=0)
    f_high, f_low = split_np(first)
    first_cat = np.concatenate([f_high, f_low, f_high], axis=1)
    angle = 2.0 * np.pi * np.outer(q, p) / NLON
    twiddle = np.concatenate([np.cos(angle), np.sin(angle)], axis=0).astype(np.float32)
    second = 2.0 * np.pi * (np.outer(high_m, p) % 128) / 128
    cos_b, sin_b = np.cos(second), np.sin(second)
    second = np.concatenate(
        [np.concatenate([cos_b, sin_b], axis=1), np.concatenate([-sin_b, cos_b], axis=1)], axis=0
    ) / math.sqrt(NLON)
    s_high, s_low = split_np(second)
    second_cat = np.concatenate([s_high, s_low], axis=0)
    return first_cat, twiddle, second_cat


def split(value):
    high = value.astype(BF16)
    low = (value - high.astype(F32)).astype(BF16)
    return high, low


def wait_bytes(ref, sem):
    pltpu.make_async_copy(ref, ref, sem).wait()


def kernel(
    fields_hbm, herm_hbm, first_hbm, twiddle_hbm, second_hbm, gath,
    fields, first_ref, twiddle_ref, second_ref, halo, xs, xr, b_hi, b_lo, zs, zr, zct, pbuf, p_hi, p_lo, zb, outs,
    halo_send, halo_recv, lon_send, lon_recv, in_send, in_recv, out_send, out_recv,
    p_send, pz_recv, px_recv, pc_recv, load, round_two,
):
    lon = lax.axis_index("lon")
    lat = lax.axis_index("lat")
    lev = lax.axis_index("lev")
    yy, core = lon // 2, lax.rem(lon, 2)
    zz, xx = lat // 4, lax.rem(lat, 4)
    half, l8 = lax.rem(lat, 2), lat // 2
    other = 1 - lev

    loads = [
        pltpu.make_async_copy(fields_hbm.at[f, 0], fields.at[f], load.at[f]) for f in (0, 5, 1, 3, 4)
    ]
    loads = dict(zip((0, 5, 1, 3, 4), loads))
    for copy in loads.values():
        copy.start()
    own_rows = pl.ds(pl.multiple_of(lat * 64, 64), 64)
    for col in range(4):
        lanes = pl.ds(pl.multiple_of(core * 512 + col * 128, 128), 128)
        pltpu.make_async_copy(herm_hbm.at[:, lanes], pbuf.at[core, col, own_rows], pc_recv.at[1]).start()
    constants = [
        pltpu.make_async_copy(hbm, ref, load.at[6 + n])
        for n, (hbm, ref) in enumerate(
            ((first_hbm, first_ref), (twiddle_hbm, twiddle_ref), (second_hbm, second_ref))
        )
    ]
    for copy in constants:
        copy.start()

    away = lax.rem(zz + 3 + 2 * lev, 4)
    partner_id = (lon, lat, other)
    away_id = (lon, away * 4 + xx, other)
    barrier = pltpu.get_barrier_semaphore()

    def greet(device_id):
        pl.semaphore_signal(barrier, inc=1, device_id=device_id, device_id_type=MESH)

    for off in range(1, 16):
        greet((lon, lax.rem(lat + off, 16), lev))
    greet(away_id)
    for off in range(1, 8):
        greet((lax.rem(lon + off, 8), lat, lev))
    for off in range(8):
        greet((lax.rem(lon + off, 8), lat, other))

    halo_copies = []
    for slot, field in enumerate((2, 4)):
        copy = pltpu.make_async_remote_copy(
            src_ref=fields_hbm.at[field, 0], dst_ref=halo.at[slot],
            send_sem=halo_send.at[slot], recv_sem=halo_recv.at[slot],
            device_id=partner_id, device_id_type=MESH,
        )
        halo_copies.append(copy)

    def make_products(dst_field, compute):
        @pl.loop(0, 8)
        def _(yb):
            rows = pl.ds(pl.multiple_of(yb * 8, 8), 8)
            value = compute(rows)
            for t in range(8):
                xs[pl.ds(dst_field * 512 + yb * 64 + t, 8, stride=8), :] = value[:, t * 128:(t + 1) * 128]

    def send_lon(step, to_core):
        field = 3 * to_core + step
        for dy in range(4):
            peer_y = lax.rem(yy + dy, 4)
            rows = pl.ds(pl.multiple_of(field * 512 + peer_y * 128, 128), 128)

            def remote():
                pltpu.make_async_remote_copy(
                    src_ref=xs.at[rows], dst_ref=xr.at[step, lon],
                    send_sem=lon_send.at[step], recv_sem=lon_recv.at[step],
                    device_id=(peer_y * 2 + to_core, lat, lev), device_id_type=MESH,
                ).start()

            if dy:
                remote()
            else:
                @pl.when(core != to_core)
                def _():
                    remote()

                @pl.when(core == to_core)
                def _():
                    pltpu.make_async_copy(xs.at[rows], xr.at[step, lon], lon_recv.at[step]).start()

    def wait_lon_sends(step):
        wait_bytes(xs.at[pl.ds(0, 896)], lon_send.at[step])

    beyond_id = (lon, away * 4 + xx, lev)
    quarter = pbuf.at[0, :, pl.ds(0, 64)]

    def rows_of(block_z, block_x, start=0, size=64):
        first = pl.multiple_of((block_z * 4 + block_x) * 64 + start, size)
        return pbuf.at[core, :, pl.ds(first, size)]

    def push(block, device_id, sem, slot):
        pltpu.make_async_remote_copy(
            src_ref=block, dst_ref=block, send_sem=p_send.at[slot], recv_sem=sem,
            device_id=device_id, device_id_type=MESH,
        ).start()

    right_id = (lon, zz * 4 + lax.rem(xx + 1, 4), lev)
    left_id = (lon, zz * 4 + lax.rem(xx + 3, 4), lev)

    def spread_x(slot, block_z):
        push(rows_of(block_z, xx), right_id, px_recv.at[slot, 0], 1)
        push(rows_of(block_z, xx), left_id, px_recv.at[slot, 1], 1)

    def relay_x(slot, block_z):
        left_x, right_x = lax.rem(xx + 3, 4), lax.rem(xx + 1, 4)
        wait_bytes(rows_of(block_z, left_x), px_recv.at[slot, 0])
        push(rows_of(block_z, left_x, 0, 32), right_id, px_recv.at[slot, 2], 3)
        wait_bytes(rows_of(block_z, right_x), px_recv.at[slot, 1])
        push(rows_of(block_z, right_x, 32, 32), left_id, px_recv.at[slot, 3], 3)

    toward = lax.rem(zz + 5 - 2 * lev, 4)
    far = lax.rem(zz + 2, 4)
    blocks = (zz, away, toward, far)

    def zonal(step):
        wait_bytes(xr.at[step], lon_recv.at[step])
        if step == 0:
            for copy in constants:
                copy.wait()
        cos_t, sin_t = twiddle_ref[0:64, :], twiddle_ref[64:128, :]

        for u in range(8):
            cats = []
            for k in range(2):
                block = xr[step, :, pl.ds(u * 16 + k * 8, 8), :].reshape(64, 128)
                high, low = split(block)
                cats.append(jnp.concatenate([high, high, low], axis=0))
            cat = jnp.concatenate(cats, axis=1)
            first = jnp.dot(first_ref[...], cat, preferred_element_type=F32)
            res, ims = [], []
            for k in range(2):
                re = first[0:64, k * 128:(k + 1) * 128]
                im = first[64:128, k * 128:(k + 1) * 128]
                res.append((re * cos_t + im * sin_t).reshape(8, 8, 128))
                ims.append((im * cos_t - re * sin_t).reshape(8, 8, 128))
            rows = pl.ds(u * 16, 16)
            for part, pair in enumerate((res, ims)):
                high, low = split(jnp.concatenate(pair, axis=1))
                b_hi[:, rows, part * 128:(part + 1) * 128] = high
                b_lo[:, rows, part * 128:(part + 1) * 128] = low

        for u in range(4):
            pair = pl.ds(u * 2, 2)
            high = b_hi[pair].reshape(256, 256)
            low = b_lo[pair].reshape(256, 256)
            nt = (((1,), (1,)), ((), ()))
            one = lax.dot_general(second_ref[...], high, nt, preferred_element_type=F32)
            two = lax.dot_general(second_ref[0:64, :], low, nt, preferred_element_type=F32)
            both = one[0:64] + one[64:128] + two
            for k in range(2):
                zs[step, :, u * 2 + k] = both[:, k * 128:(k + 1) * 128].reshape(8, 8, 128)

    source = lat * 4 + yy
    my_g, my_s = source // 8, lax.rem(source, 8)

    to_x = [lax.rem(xx + 2 * dx, 4) // 2 * 2 + core for dx in range(2)]
    to_lats = {(dz, dx): lax.rem(zz + dz, 4) * 4 + to_x[dx] for dz in range(4) for dx in range(2)}
    to_l8 = {key: value // 2 for key, value in to_lats.items()}
    crossed = jnp.where(core == 1, other, lev)

    def send_in(step):
        to_lev = crossed if step else lev

        @pl.loop(0, 8)
        def _(k):
            to_lon = lax.rem(lon + k, 8)
            for dz in (2, 1, 3, 0):
                for dx in range(2):
                    to_lat = to_lats[dz, dx]
                    src = zs.at[step, to_lon, to_l8[dz, dx]]
                    dst = zr.at[step, my_g, my_s]

                    def remote():
                        pltpu.make_async_remote_copy(
                            src_ref=src, dst_ref=dst,
                            send_sem=in_send.at[step], recv_sem=in_recv.at[step],
                            device_id=(to_lon, to_lat, to_lev), device_id_type=MESH,
                        ).start()

                    if dz or dx:
                        remote()
                        continue
                    mine = jnp.logical_and(
                        jnp.logical_and(k == 0, to_lat == lat), to_lev == lev
                    )

                    @pl.when(jnp.logical_not(mine))
                    def _():
                        remote()

                    @pl.when(mine)
                    def _():
                        pltpu.make_async_copy(src, dst, in_recv.at[step]).start()

    def wait_in_sends(step):
        flip = jnp.logical_and(core == 1, step >= 1)
        has_self = jnp.logical_and(half == core, jnp.logical_not(flip))

        @pl.when(has_self)
        def _():
            wait_bytes(zs.at[step, pl.ds(0, 7)], in_send.at[step])
            wait_bytes(zs.at[step, 0, pl.ds(0, 7)], in_send.at[step])

        @pl.when(jnp.logical_not(has_self))
        def _():
            wait_bytes(zs.at[step], in_send.at[step])

    def send_round_two():
        for off in range(1, 16):
            pl.semaphore_signal(
                round_two, inc=1, device_id=(lon, lax.rem(lat + off, 16), lev), device_id_type=MESH
            )

    loads[0].wait()
    loads[5].wait()
    make_products(0, lambda r: fields[0, r, :] * fields[5, r, :])
    loads[1].wait()
    loads[3].wait()
    make_products(3, lambda r: fields[1, r, :] * fields[3, r, :])
    pl.semaphore_wait(barrier, 31)
    for copy in halo_copies:
        copy.start()
    send_lon(0, 0)
    send_lon(0, 1)
    send_round_two()
    wait_bytes(quarter, pc_recv.at[1])
    push(rows_of(zz, xx), away_id, pz_recv.at[0], 0)
    push(rows_of(zz, xx), beyond_id, pz_recv.at[1], 0)
    spread_x(0, zz)
    make_products(1, lambda r: fields[0, r, :] * fields[1, r, :])
    loads[4].wait()
    make_products(2, lambda r: fields[0, r, :] * fields[4, r, :])
    sign = jnp.where(lev == 0, F32(-0.5), F32(0.5))
    send_lon(1, 0)
    wait_bytes(quarter, pz_recv.at[1])
    push(rows_of(toward, xx), away_id, pz_recv.at[2], 0)
    spread_x(2, toward)
    wait_bytes(quarter, pz_recv.at[0])
    spread_x(1, away)
    halo_copies[0].wait_recv()
    make_products(4, lambda r: halo[0, r, :] * (fields[0, r, :] * sign))
    send_lon(1, 1)
    zonal(0)
    pl.semaphore_wait(round_two, 15)
    send_in(0)
    relay_x(0, blocks[0])
    halo_copies[1].wait_recv()
    make_products(
        5,
        lambda r: halo[0, r, :] * (fields[3, r, :] * sign)
        - 0.25 * (fields[4, r, :] - 2.0 * halo[1, r, :]),
    )
    wait_lon_sends(1)
    send_lon(2, 0)
    send_lon(2, 1)
    wait_bytes(quarter, pz_recv.at[2])
    spread_x(3, far)
    relay_x(2, blocks[2])
    relay_x(1, blocks[1])
    zonal(1)
    send_in(1)
    relay_x(3, blocks[3])
    zonal(2)
    send_in(2)

    for slot in range(4):
        for side in range(2):
            wait_bytes(pbuf.at[0, :, pl.ds(0, 32)], px_recv.at[slot, 2 + side])
    to_sibling = pltpu.make_async_remote_copy(
        src_ref=pbuf.at[core], dst_ref=pbuf.at[core],
        send_sem=p_send.at[2], recv_sem=pc_recv.at[0],
        device_id=(lon + 1 - 2 * core, lat, lev), device_id_type=MESH,
    )
    to_sibling.start()

    def prepare(which):
        @pl.loop(0, 8)
        def _(g):
          for u in range(8):
            for col in range(4):
                pieces = [
                    pbuf[which, col, pl.ds(g * 128 + u * 2 + k, 8, stride=16), :]
                    for k in range(2)
                ]
                high, low = split(jnp.concatenate(pieces, axis=0))
                rows = pl.ds(pl.multiple_of(g * 128 + u * 16, 16), 16)
                p_hi[which, rows, col * 128:(col + 1) * 128] = high
                p_lo[which, rows, col * 128:(col + 1) * 128] = low

    lane = lax.broadcasted_iota(jnp.int32, (64, 128), 1)
    low_lanes = lax.broadcasted_iota(jnp.int32, (32, 128), 1) < 64

    def transpose_in(step):
        wait_bytes(zr.at[step], in_recv.at[step])
        v = [zr[step, :, s].reshape(64, 128) for s in range(8)]
        for k in range(3):
            bit = 1 << k
            low_half = (lane & bit) == 0
            new = list(v)
            for a in range(8):
                if a & bit:
                    continue
                b = a | bit
                new[a] = jnp.where(low_half, v[a], pltpu.roll(v[b], bit, 1))
                new[b] = jnp.where(low_half, pltpu.roll(v[a], 128 - bit, 1), v[b])
            v = new
        for j in range(8):
            for g in range(8):
                zct[g, pl.ds(j, 8, stride=8), :] = v[j][g * 8:(g + 1) * 8]
        high, low = split(jnp.concatenate([zct[g] for g in range(8)], axis=1))
        zb[0:64, :] = high
        zb[64:128, :] = low

    def project(step, which):
        for col in range(2):
            cols = slice(col * 256, (col + 1) * 256)
            one = jnp.dot(zb[...], p_hi[which, :, cols], preferred_element_type=F32)
            two = jnp.dot(zb[0:64, :], p_lo[which, :, cols], preferred_element_type=F32)
            both = one[0:64] + one[64:128] + two
            for k in range(2):
                t = which * 4 + col * 2 + k
                a = both[0:32, k * 128:(k + 1) * 128]
                b = both[32:64, k * 128:(k + 1) * 128]
                even = jnp.where(low_lanes, a, pltpu.roll(b, 64, 1))
                odd = jnp.where(low_lanes, pltpu.roll(a, 64, 1), b)
                outs[step, 2 * t] = even.reshape(4, 8, 128)
                outs[step, 2 * t + 1] = odd.reshape(4, 8, 128)

        for j in range(8):
            to_lat = which * 8 + lax.rem(lat + 2 + j, 8)

            @pl.when(to_lat != lat)
            def _():
                pltpu.make_async_remote_copy(
                    src_ref=outs.at[step, to_lat], dst_ref=gath.at[step, half, :, l8],
                    send_sem=out_send.at[step], recv_sem=out_recv.at[step],
                    device_id=(lon, to_lat, lev), device_id_type=MESH,
                ).start()

            @pl.when(to_lat == lat)
            def _():
                pltpu.make_async_copy(
                    outs.at[step, to_lat], gath.at[step, half, :, l8], out_recv.at[step]
                ).start()

    prepare(core)
    transpose_in(0)
    project(0, core)
    wait_bytes(pbuf.at[0], pc_recv.at[0])
    prepare(1 - core)
    project(0, 1 - core)
    transpose_in(1)
    project(1, core)
    project(1, 1 - core)
    transpose_in(2)
    project(2, core)
    project(2, 1 - core)

    for step in range(STEPS):
        wait_bytes(gath.at[step], out_recv.at[step])

    wait_lon_sends(2)
    wait_lon_sends(0)
    for copy in halo_copies:
        copy.wait_send()
    for step in range(STEPS):
        wait_in_sends(step)
        wait_bytes(outs.at[step, pl.ds(0, 15)], out_send.at[step])
    wait_bytes(pbuf.at[0, :, pl.ds(0, 192)], p_send.at[0])
    wait_bytes(pbuf.at[0, :, pl.ds(0, 512)], p_send.at[1])
    wait_bytes(pbuf.at[0, :, pl.ds(0, 256)], p_send.at[3])
    to_sibling.wait_send()


def assemble(gath_hbm, out_ref, gath, load):
    copies = [
        pltpu.make_async_copy(gath_hbm.at[step], gath.at[step], load.at[step]) for step in range(STEPS)
    ]
    for copy in copies:
        copy.start()
    for step in range(STEPS):
        copies[step].wait()
        for half in range(2):
            field = 3 * half + step
            for t in range(2):
                turned = gath[step, half, 2 * t:2 * t + 2].reshape(128, 128).T
                for h in range(2):
                    sb = 2 * h + t
                    for n0 in range(0, 64, 8):
                        out_ref[pl.ds((n0 * 6 + field) * 4 + sb, 8, stride=24), :] = (
                            turned[h * 64 + n0:h * 64 + n0 + 8]
                        )


def on_device(fields_grid, hermite_proj):
    first_cat, twiddle, second_cat = tables()
    hbm = pl.BlockSpec(memory_space=pltpu.HBM)
    dma = pltpu.SemaphoreType.DMA
    gathered = pl.pallas_call(
        kernel,
        out_shape=jax.ShapeDtypeStruct((3, 2, 4, 8, 8, 128), F32),
        in_specs=[hbm] * 5,
        out_specs=hbm,
        scratch_shapes=[
            pltpu.VMEM((6, 64, 1024), F32),
            pltpu.VMEM((128, 192), BF16),
            pltpu.VMEM((128, 128), F32),
            pltpu.VMEM((128, 256), BF16),
            pltpu.VMEM((2, 64, 1024), F32),
            pltpu.VMEM((6 * 512, 128), F32),
            pltpu.VMEM((3, 8, 128, 128), F32),
            pltpu.VMEM((8, 128, 256), BF16),
            pltpu.VMEM((8, 128, 256), BF16),
            pltpu.VMEM((3, 8, 8, 8, 128), F32),
            pltpu.VMEM((3, 8, 8, 8, 128), F32),
            pltpu.VMEM((8, 64, 128), F32),
            pltpu.VMEM((2, 4, 1024, 128), F32),
            pltpu.VMEM((2, 1024, 512), BF16),
            pltpu.VMEM((2, 1024, 512), BF16),
            pltpu.VMEM((128, 1024), BF16),
            pltpu.VMEM((3, 16, 4, 8, 128), F32),
            dma((2,)), dma((2,)), dma((3,)), dma((3,)), dma((3,)), dma((3,)), dma((3,)), dma((3,)),
            dma((4,)), dma((3,)), dma((4, 4)), dma((2,)), dma((9,)),
            pltpu.SemaphoreType.REGULAR,
        ],
        compiler_params=pltpu.CompilerParams(
            collective_id=0, has_side_effects=True, vmem_limit_bytes=60 * 1024 * 1024
        ),
    )(fields_grid, hermite_proj, first_cat, twiddle, second_cat)
    out = pl.pallas_call(
        assemble,
        out_shape=jax.ShapeDtypeStruct((1536, 128), F32),
        in_specs=[hbm],
        out_specs=pl.BlockSpec(memory_space=pltpu.VMEM),
        scratch_shapes=[pltpu.VMEM((3, 2, 4, 8, 8, 128), F32), dma((3,))],
        compiler_params=pltpu.CompilerParams(vmem_limit_bytes=60 * 1024 * 1024),
    )(gathered)
    return out.reshape(64, 6, 1, 512)


def solution(mesh):
    in_specs = (P(None, "lev", "lat", "lon"), P("lat", None))
    out_specs = P("lat", None, "lev", "lon")
    return jax.shard_map(
        on_device, mesh=mesh, in_specs=in_specs, out_specs=out_specs, check_vma=False
    )
```
